512 devices in a mesh: row: 16 (over z, y_lo), col: 32 (over y_hi, x, core).
Axes of the slice: x: 4, y: 8 (y_hi: 4, y_lo: 2; y = y_hi * 2 + y_lo), z: 8, core: 2. Of those that a mesh axis runs over, the one named last changes fastest.
Arguments:
- x_feat: bfloat16 [65536, 256], P('col', 'row'), may hold values from -6 to 6
- weight: bfloat16 [256, 256], replicated, may hold values from -0.375 to 0.375
- tile_vals: bfloat16 [16, 32, 96, 128, 128], P('row', 'col'), may hold values from -0.0546875 to 0.0546875
- tile_row: int32 [16, 32, 96], P('row', 'col'), may hold values from 0 to 31
- tile_col: int32 [16, 32, 96], P('row', 'col'), may hold values from 0 to 15
- tile_live: int32 [16, 32, 96], P('row', 'col'), may hold values from 0 to 1, as said below
- d_out: bfloat16 [65536, 256], P(('row', 'col')), may hold values from -6 to 6
Outputs:
- layer_out: bfloat16 [65536, 256], P(('row', 'col'))
- weight_grad: float32 [256, 256], replicated
- feat_grad: bfloat16 [65536, 256], P('col', 'row')
The draws below stay inside these ranges and needn't reach their ends.
Inputs may be any that keep to these rules, and one draw needn't show every extreme that they name: `tile_live`: every device has at least max(24, 1) live slots, and in every draw some device has all 96 live.
All inputs are finite; a program needn't handle non-finite values.
Results may differ from the reference program's by a relative error of at most 0.024.
Values may be sent and summed in bfloat16 or wider, within the bound.
A program may use at most 64 MiB of HBM per device.

```python
import math
import jax
import jax.numpy as jnp
import numpy as np
from jax import lax

F = 256
TILE = 128
CB = 2048
SLOTS = 96
RB = 4096
NODES = 65536
N_ROW = 16
N_COL = 32


def draw_tile_live(key, part):
    key = jax.random.fold_in(key, 5)
    key_count, key_full, key_order = jax.random.split(key, 3)
    lowest = max(SLOTS // 4, 1)
    counts = jax.random.randint(key_count, (N_ROW * N_COL,), lowest, SLOTS + 1)
    chosen = jax.random.randint(key_full, (), 0, N_ROW * N_COL)
    counts = jnp.where(jnp.arange(N_ROW * N_COL) == chosen, SLOTS, counts).reshape(N_ROW, N_COL)
    scores = jax.random.randint(key_order, (N_ROW, N_COL, SLOTS), 0, 2 ** 20) * SLOTS + jnp.arange(SLOTS, dtype=jnp.int32)
    ranks = jnp.argsort(jnp.argsort(scores, axis=-1), axis=-1)
    return (ranks < counts[:, :, None]).astype(jnp.int32)


def set_ends(drawn, stream_key, low, top_value):
    index_at = [jax.random.randint(jax.random.fold_in(stream_key, axis), (), 0, length) for axis, length in enumerate(drawn.shape)]
    widest = drawn.shape.index(max(drawn.shape))
    beside = index_at[:widest] + [(index_at[widest] + 1) % drawn.shape[widest]] + index_at[widest + 1:]
    return drawn.at[tuple(index_at)].set(low).at[tuple(beside)].set(top_value)


def steps_of(key, dims, pieces, least, top_value):
    loudness, own = 1.0, jax.random.fold_in(key, 6)
    for dim, shards_of in pieces:
        draws = jnp.exp(jax.random.uniform(jax.random.fold_in(own, dim), (shards_of,), jnp.float32, least / len(pieces), top_value / len(pieces)))
        loudness = loudness * jnp.repeat(draws, dims[dim] // shards_of).reshape([-1 if axis == dim else 1 for axis in range(len(dims))])
    return loudness


def rank_bounds(amount, skew):
    loads = [(1 << 20) // math.isqrt(standing ** skew) + 1 for standing in range(1, amount + 1)]
    scale = 1 + sum(loads) // (1 << 30)
    return np.cumsum(np.array([max(1, weight // scale) for weight in loads]))


def ranked_ids(key, shape, count, lean):
    listing = rank_bounds(count, lean)
    ticket = jax.random.randint(jax.random.fold_in(key, 1), shape, 0, int(listing[count - 1]))
    standing = jnp.searchsorted(jnp.asarray(listing, jnp.int32), ticket, side="right")
    return jax.random.permutation(jax.random.fold_in(key, 2), count)[standing].astype(jnp.int32)


def normal_values(own_key, shape, spread, reach, shards=(), held_as=jnp.bfloat16):
    result = spread * jax.random.normal(own_key, shape, jnp.float32)
    if shards:
        result = result * steps_of(own_key, shape, shards, -0.22, 0.18)
    return jnp.clip(result, -reach, reach).astype(held_as)


def setup_inputs(seed: int = 0) -> dict:
    arg_keys = jax.random.split(jax.random.key(seed), 8)
    x_feat = normal_values(arg_keys[0], (NODES, F), 1.0, 6.0, ((0, 32), (1, 16)))
    weight = normal_values(arg_keys[1], (F, F), F ** -0.5, 0.375)
    tile_vals = normal_values(arg_keys[2], (N_ROW, N_COL, SLOTS, TILE, TILE), (SLOTS * N_COL * TILE * TILE // RB) ** -0.5, 0.0546875, ((0, 16), (1, 32)))
    tile_row = set_ends(ranked_ids(arg_keys[3], (N_ROW, N_COL, SLOTS), RB // TILE, 1), jax.random.fold_in(arg_keys[3], 3), 0, (RB // TILE) - 1).astype(jnp.int32)
    tile_col = set_ends(jax.random.randint(arg_keys[4], (N_ROW, N_COL, SLOTS), 0, CB // TILE), jax.random.fold_in(arg_keys[4], 1), 0, (CB // TILE) - 1).astype(jnp.int32)
    tile_live = draw_tile_live(jax.random.fold_in(arg_keys[7], 71), 0)
    d_out = normal_values(arg_keys[6], (NODES, F), 1.0, 6.0, ((0, 512),))
    return {"x_feat": x_feat, "weight": weight, "tile_vals": tile_vals, "tile_row": tile_row, "tile_col": tile_col, "tile_live": tile_live, "d_out": d_out}


def local_product(vals, trow, tcol, live, feats, nout, transpose):
    width = feats.shape[1]
    ftiles = feats.astype(jnp.float32).reshape(-1, TILE, width)
    vals32 = vals.astype(jnp.float32)
    if transpose:
        picked = jnp.take(ftiles, trow, axis=0)
        prods = jnp.einsum('sji,sjf->sif', vals32, picked)
        target = tcol
    else:
        picked = jnp.take(ftiles, tcol, axis=0)
        prods = jnp.einsum('sij,sjf->sif', vals32, picked)
        target = trow
    onehot = ((target[None, :] == jnp.arange(nout, dtype=jnp.int32)[:, None]) & (live[None, :] > 0)).astype(jnp.float32)
    return jnp.einsum('ts,sif->tif', onehot, prods).reshape(nout * TILE, width)

def reference(x_feat, weight, tile_vals, tile_row, tile_col, tile_live, d_out):
    trows = RB // TILE
    tcols = CB // TILE
    xblocks = x_feat.reshape(N_COL, CB, F)

    def forward_row(r):

        def over_c(acc, c):
            part = local_product(tile_vals[r, c], tile_row[r, c], tile_col[r, c], tile_live[r, c], xblocks[c], trows, False)
            rounded = lax.optimization_barrier(part.astype(jnp.bfloat16))
            return (acc + rounded.astype(jnp.float32), None)
        acc, _ = lax.scan(over_c, jnp.zeros((RB, F), jnp.float32), jnp.arange(N_COL, dtype=jnp.int32))
        return acc
    agg = lax.map(forward_row, jnp.arange(N_ROW, dtype=jnp.int32)).reshape(NODES, F).astype(jnp.bfloat16)
    layer_out = jnp.dot(agg, weight, preferred_element_type=jnp.float32).astype(jnp.bfloat16)
    d_agg = jnp.dot(d_out, weight.T, preferred_element_type=jnp.float32).astype(jnp.bfloat16)
    weight_grad = jnp.dot(agg.T, d_out, preferred_element_type=jnp.float32) * (1.0 / math.sqrt(NODES))
    gblocks = d_agg.reshape(N_ROW, RB, F)

    def backward_col(c):

        def over_r(acc, r):
            part = local_product(tile_vals[r, c], tile_row[r, c], tile_col[r, c], tile_live[r, c], gblocks[r], tcols, True)
            return (acc + part, None)
        acc, _ = lax.scan(over_r, jnp.zeros((CB, F), jnp.float32), jnp.arange(N_ROW, dtype=jnp.int32))
        return acc
    feat_grad = lax.map(backward_col, jnp.arange(N_COL, dtype=jnp.int32)).reshape(NODES, F).astype(jnp.bfloat16)
    return (layer_out, weight_grad, feat_grad)
```

```python
import functools
import math

import jax
import jax.numpy as jnp
from jax import lax
from jax.experimental import pallas as pl
from jax.experimental.pallas import tpu as pltpu
from jax.sharding import PartitionSpec as P

TILE = 128
F = 256
NZ, NYL = 8, 2
NYH, NX, NK = 4, 4, 2
N_ROW, N_COL = NZ * NYL, NYH * NX * NK
SLOTS = 96
TR, TC = 32, 16
BF = jnp.bfloat16
F32 = jnp.float32
MESH = pl.DeviceIdType.MESH


def place():
    row, col = lax.axis_index("row"), lax.axis_index("col")
    return row // NYL, row % NYL, col // (NX * NK), (col // NK) % NX, col % NK


class Wire:
    def __init__(self, send, recv):
        self.send, self.recv, self.used, self.started = send, recv, 0, []

    def slot(self):
        self.used += 1
        return self.used - 1

    def start(self, slot, src, dst, device):
        copy = pltpu.make_async_remote_copy(
            src_ref=src, dst_ref=dst, send_sem=self.send.at[slot], recv_sem=self.recv.at[slot],
            device_id=device, device_id_type=MESH)
        copy.start()
        self.started.append(copy)

    def landed(self, slot, dst, device):
        pltpu.make_async_remote_copy(
            src_ref=dst, dst_ref=dst, send_sem=self.send.at[slot], recv_sem=self.recv.at[slot],
            device_id=device, device_id_type=MESH).wait_recv()

    def drain(self):
        for copy in self.started:
            copy.wait_send()


def devices_around():
    z, yl, yh, x, k = place()

    def at(dz=0, dyl=0, dyh=0, dx=0, dk=0):
        row = ((z + dz) % NZ) * NYL + (yl + dyl) % NYL
        col = (((yh + dyh) % NYH) * NX + (x + dx) % NX) * NK + (k + dk) % NK
        return row, col

    return at


N_GATHER = 1 + 16 + 4 + 16 + 16


def gather_kernel(x_ref, d_ref, xg, dg, send, recv):
    z, yl, yh, x, k = place()
    at = devices_around()
    me = at()
    wire = Wire(send, recv)
    zdev = {1: at(dz=1), -1: at(dz=-1)}
    xdev = {1: at(dx=1), -1: at(dx=-1)}
    ydev = {1: at(dyh=1), -1: at(dyh=-1)}
    sib, ylo = at(dk=1), at(dyl=1)
    barrier = pltpu.get_barrier_semaphore()
    around = [zdev[1], zdev[-1], xdev[1], xdev[-1], ydev[1], ydev[-1], sib, ylo]
    for device in around:
        pl.semaphore_signal(barrier, inc=1, device_id=device, device_id_type=MESH)
    pl.semaphore_wait(barrier, len(around))

    ys = wire.slot()
    zs = {(d, s, u): wire.slot() for d in (1, -1) for s in (1, 2, 3, 4) for u in (0, 1)}
    half = {1: pl.ds(0, TC // 2), -1: pl.ds(TC // 2, TC // 2)}

    def xchunk(dz, u):
        return xg.at[at(dz=dz, dyl=u)[0]]

    def xpart(dz, u, d, s):
        ref = xchunk(dz, u)
        return ref.at[half[d]] if s == 4 else ref

    def z_send(d, s, u, src=None):
        dst = xpart(-d * (s - 1), u, d, s)
        wire.start(zs[d, s, u], dst if src is None else src, dst, zdev[d])

    def z_landed(d, s, u):
        wire.landed(zs[d, s, u], xpart(-d * s, u, d, s), zdev[-d])

    def piece(j, dx=0, dk=0):
        return dg.at[at(dyh=j, dx=dx, dk=dk)[1]]

    rows = {1: pl.ds(0, TILE // 2), -1: pl.ds(TILE // 2, TILE // 2)}
    y1 = {d: wire.slot() for d in (1, -1)}
    y2 = {d: wire.slot() for d in (1, -1)}
    x1 = {(d, j): wire.slot() for d in (1, -1) for j in range(4)}
    x2 = {(d, j): wire.slot() for d in (1, -1) for j in range(4)}
    ks = {(j, dx): wire.slot() for j in range(4) for dx in range(4)}

    def to_x(j, src=None):
        for d in (1, -1):
            wire.start(x1[d, j], piece(j) if src is None else src, piece(j), xdev[d])

    def to_sib(j, dx, src=None):
        wire.start(ks[j, dx % 4], piece(j, dx) if src is None else src, piece(j, dx), sib)

    def x1_landed(j):
        for d in (1, -1):
            wire.landed(x1[d, j], piece(j, -d), xdev[-d])
            part = piece(j, -d).at[rows[d]]
            wire.start(x2[d, j], part, part, xdev[d])
            to_sib(j, -d)

    def x2_landed(j):
        for d in (1, -1):
            wire.landed(x2[d, j], piece(j, 2).at[rows[d]], xdev[-d])
        to_sib(j, 2)

    wire.start(ys, x_ref, xchunk(0, 0), ylo)
    for d in (1, -1):
        z_send(d, 1, 0, x_ref)
    for d in (1, -1):
        wire.start(y1[d], d_ref, piece(0), ydev[d])
    to_x(0, d_ref)
    to_sib(0, 0, d_ref)
    xg[me[0]] = x_ref[...]
    dg[me[1]] = d_ref[...]

    wire.landed(ys, xchunk(0, 1), ylo)
    for d in (1, -1):
        z_send(d, 1, 1)
    for d in (1, -1):
        wire.landed(y1[d], piece(-d), ydev[-d])
        part = piece(-d).at[rows[d]]
        wire.start(y2[d], part, part, ydev[d])
        to_x(-d % 4)
        to_sib(-d % 4, 0)
    for u in (0, 1):
        for d in (1, -1):
            z_landed(d, 1, u)
            z_send(d, 2, u)
    x1_landed(0)
    for d in (1, -1):
        wire.landed(y2[d], piece(2).at[rows[d]], ydev[-d])
    to_x(2)
    to_sib(2, 0)
    x1_landed(3)
    x1_landed(1)
    for u in (0, 1):
        for d in (1, -1):
            z_landed(d, 2, u)
            z_send(d, 3, u)
    x2_landed(0)
    x1_landed(2)
    x2_landed(3)
    x2_landed(1)
    for u in (0, 1):
        for d in (1, -1):
            z_landed(d, 3, u)
            z_send(d, 4, u)
    x2_landed(2)
    for u in (0, 1):
        for d in (1, -1):
            z_landed(d, 4, u)
    for j in range(4):
        for dx in range(4):
            wire.landed(ks[j, dx], piece(j, dx, 1), sib)
    wire.drain()


def gather(xt, d_out):
    vmem = pl.BlockSpec(memory_space=pltpu.VMEM)
    return pl.pallas_call(
        gather_kernel,
        out_shape=(
            jax.ShapeDtypeStruct((N_ROW, TC, F // N_ROW, TILE), BF),
            jax.ShapeDtypeStruct((N_COL, TILE, F), BF),
        ),
        in_specs=[vmem] * 2,
        out_specs=(vmem, vmem),
        scratch_shapes=[pltpu.SemaphoreType.DMA((N_GATHER,)), pltpu.SemaphoreType.DMA((N_GATHER,))],
        compiler_params=pltpu.CompilerParams(
            collective_id=0, has_side_effects=True, vmem_limit_bytes=24 << 20),
        name="gather",
    )(xt, d_out)


UNROLL = 8


def cell_kernel(trow, tcol, live, vals, xg, dg, w, pt, bt, g, acc_p, acc_b, gt):
    acc_p[...] = jnp.zeros_like(acc_p)
    acc_b[...] = jnp.zeros_like(acc_b)
    contract = (((1,), (1,)), ((), ()))

    def forward(i, carry):
        for v in range(UNROLL):
            s = i * UNROLL + v
            target = jnp.where(live[s] > 0, trow[s], TR)
            xt = xg[:, tcol[s]].reshape(F, TILE)
            acc_p[target] += lax.dot_general(xt, vals[s], contract, preferred_element_type=F32)
        return carry

    lax.fori_loop(0, SLOTS // UNROLL, forward, 0)

    def grads(i, carry):
        for v in range(UNROLL):
            t = i * UNROLL + v
            gt[t] = lax.dot_general(w[...], dg[t], contract, preferred_element_type=F32).astype(BF)
        return carry

    lax.fori_loop(0, TR // UNROLL, grads, 0)

    def backward(i, carry):
        for v in range(UNROLL):
            s = i * UNROLL + v
            target = jnp.where(live[s] > 0, tcol[s], TC)
            acc_b[target] += jnp.dot(gt[trow[s]], vals[s], preferred_element_type=F32)
        return carry

    lax.fori_loop(0, SLOTS // UNROLL, backward, 0)

    def finish(i, total):
        for v in range(UNROLL):
            t = i * UNROLL + v
            tile = acc_p[t].astype(BF)
            pt[t] = tile
            total += jnp.dot(tile, dg[t], preferred_element_type=F32)
        return total

    total = lax.fori_loop(0, TR // UNROLL, finish, jnp.zeros((F, F), F32)).astype(BF)
    for q in range(N_COL):
        a, h = q // 2, q % 2
        g[q] = total[a * 16:(a + 1) * 16, h * TILE:(h + 1) * TILE]

    def spread(i, carry):
        bt[:, i] = acc_b[i].astype(BF).reshape(N_ROW, F // N_ROW, TILE)
        return carry

    lax.fori_loop(0, TC, spread, 0)


def cell(trow, tcol, live, vals, xg, dg, w):
    vmem = pl.BlockSpec(memory_space=pltpu.VMEM)
    smem = pl.BlockSpec(memory_space=pltpu.SMEM)
    return pl.pallas_call(
        cell_kernel,
        out_shape=(
            jax.ShapeDtypeStruct((N_COL, F, TILE), BF),
            jax.ShapeDtypeStruct((N_ROW, TC, F // N_ROW, TILE), BF),
            jax.ShapeDtypeStruct((N_COL, 16, TILE), BF),
        ),
        in_specs=[smem] * 3 + [vmem] * 4,
        out_specs=(vmem, vmem, vmem),
        scratch_shapes=[
            pltpu.VMEM((TR + 1, F, TILE), F32),
            pltpu.VMEM((TC + 1, F, TILE), F32),
            pltpu.VMEM((TR, F, TILE), BF),
        ],
        compiler_params=pltpu.CompilerParams(vmem_limit_bytes=40 << 20),
        name="cell",
    )(trow, tcol, live, vals, xg, dg, w)


N_REDUCE = 4 + 8 + 8 + 2 + 2 + 16 + 1


def total_of(refs):
    out = refs[0][...].astype(F32)
    for ref in refs[1:]:
        out += ref[...].astype(F32)
    return out.astype(BF)


def reduce_kernel(scale, pt, bt, g, w, layer, feat, wgrad,
                  gall, core_in, c, x1p, x1m, x2p, x2m, dsum, y1p, y1m, y2p, y2m,
                  bp, bm, e, ylr, g_in, g_sum, g_row, g_tot, send, recv, gsend, grecv):
    z, yl, yh, x, k = place()
    at = devices_around()
    row, col = at()
    wire = Wire(send, recv)
    zdev = {1: at(dz=1), -1: at(dz=-1)}
    xdev = {1: at(dx=1), -1: at(dx=-1)}
    ydev = {1: at(dyh=1), -1: at(dyh=-1)}
    sib, ylo = at(dk=1), at(dyl=1)
    barrier = pltpu.get_barrier_semaphore()

    def greet_col(o, carry):
        pl.semaphore_signal(barrier, inc=1, device_id=(row, (col + o) % N_COL), device_id_type=MESH)
        return carry

    def greet_row(o, carry):
        pl.semaphore_signal(barrier, inc=1, device_id=((row + o) % N_ROW, col), device_id_type=MESH)
        return carry

    lax.fori_loop(1, N_COL, greet_col, 0)
    lax.fori_loop(1, N_ROW, greet_row, 0)
    pl.semaphore_wait(barrier, N_COL + N_ROW - 2)

    x1b, x2b = {1: x1p, -1: x1m}, {1: x2p, -1: x2m}
    y1b, y2b = {1: y1p, -1: y1m}, {1: y2p, -1: y2m}
    bb = {1: bp, -1: bm}
    near = {1: pl.ds(0, TILE), -1: pl.ds(TILE, TILE)}
    far = {1: near[-1], -1: near[1]}
    bnear = {1: pl.ds(0, TC // 2), -1: pl.ds(TC // 2, TC // 2)}
    bfar = {1: bnear[-1], -1: bnear[1]}

    def yy(j):
        return (yh + j) % NYH

    order = (2, 1, 3, 0)
    cs = {j: wire.slot() for j in order}
    xs1 = {(d, j): wire.slot() for d in (1, -1) for j in order}
    xs2 = {(d, j): wire.slot() for d in (1, -1) for j in order}
    ys1 = {d: wire.slot() for d in (1, -1)}
    ys2 = {d: wire.slot() for d in (1, -1)}
    bs = {(d, s, u): wire.slot() for d in (1, -1) for s in (0, 1, 2, 3) for u in (0, 1)}
    yls = wire.slot()

    def bt_at(dz, u):
        return bt.at[at(dz=dz, dyl=u)[0]]

    def b_send(d, s, u):
        if s == 0:
            wire.start(bs[d, s, u], bt_at(4, u).at[bnear[d]], bb[d].at[0, u, bnear[d]], zdev[d])
        else:
            wire.start(bs[d, s, u], bb[d].at[s - 1, u], bb[d].at[s, u], zdev[d])

    def b_add(d, s, u):
        own = bt_at(d * (3 - s), u)
        if s == 0:
            landing = bb[d].at[0, u, bnear[d]]
            bb[d][0, u, bfar[d]] = own[bfar[d]]
            wire.landed(bs[d, s, u], landing, zdev[-d])
            bb[d][0, u, bnear[d]] = total_of([landing, own.at[bnear[d]]])
        else:
            landing = bb[d].at[s, u]
            wire.landed(bs[d, s, u], landing, zdev[-d])
            bb[d][s, u] = total_of([landing, own])
        b_send(d, s + 1, u)

    def b_step(s):
        for u in (1, 0):
            for d in (1, -1):
                b_add(d, s, u)

    for j in order:
        wire.start(cs[j], pt.at[yy(j), :, 1 - k], core_in.at[yy(j)], sib)
    for u in (1, 0):
        for d in (1, -1):
            b_send(d, 0, u)

    def g_out(o, carry):
        to = (col + o) % N_COL
        pltpu.make_async_remote_copy(
            src_ref=g.at[to], dst_ref=g_in.at[o - 1], send_sem=gsend.at[0], recv_sem=grecv.at[0],
            device_id=(row, to), device_id_type=MESH).start()
        return carry

    lax.fori_loop(1, N_COL, g_out, 0)

    for j in order:
        wire.landed(cs[j], core_in.at[yy(j)], sib)

        def add(i, carry):
            c[yy(j), i] = total_of([pt.at[yy(j), i, k], core_in.at[yy(j), i]])
            return carry

        lax.fori_loop(0, NX, add, 0)
        for d in (1, -1):
            wire.start(xs1[d, j], c.at[yy(j), (x + 2) % NX, near[d]], x1b[d].at[j, near[d]], xdev[d])

    b_step(0)

    pltpu.make_async_copy(g_in, g_in, grecv.at[0]).wait()
    g_sum[...] = (jnp.sum(g_in[...].astype(F32), axis=0) + g[col].astype(F32)).astype(BF)

    def g_rows(o, carry):
        to = (row + o) % N_ROW
        pltpu.make_async_remote_copy(
            src_ref=g_sum, dst_ref=g_row.at[o - 1], send_sem=gsend.at[1], recv_sem=grecv.at[1],
            device_id=(to, col), device_id_type=MESH).start()
        return carry

    lax.fori_loop(1, N_ROW, g_rows, 0)

    for j in order:
        for d in (1, -1):
            own = c.at[yy(j), (x + d) % NX]
            x1b[d][j, far[d]] = own[far[d]]
            landing = x1b[d].at[j, near[d]]
            wire.landed(xs1[d, j], landing, xdev[-d])
            x1b[d][j, near[d]] = total_of([landing, own.at[near[d]]])
            wire.start(xs2[d, j], x1b[d].at[j], x2b[d].at[j], xdev[d])

    b_step(1)

    pltpu.make_async_copy(g_row, g_row, grecv.at[1]).wait()
    g_tot[...] = (jnp.sum(g_row[...].astype(F32), axis=0) + g_sum[...].astype(F32)).astype(BF)
    gall[0] = g_tot[...]

    def g_back(o, carry):
        to = (col + o) % N_COL
        pltpu.make_async_remote_copy(
            src_ref=g_tot, dst_ref=gall.at[o], send_sem=gsend.at[2], recv_sem=grecv.at[2],
            device_id=(row, to), device_id_type=MESH).start()
        return carry

    lax.fori_loop(1, N_COL, g_back, 0)

    for j in order:
        for d in (1, -1):
            wire.landed(xs2[d, j], x2b[d].at[j], xdev[-d])
        dsum[j] = total_of([c.at[yy(j), x], x2p.at[j], x2m.at[j]])
        if j == 2:
            for d in (1, -1):
                wire.start(ys1[d], dsum.at[2, near[d]], y1b[d].at[near[d]], ydev[d])
        if j in (1, 3):
            d = 1 if j == 1 else -1
            y1b[d][far[d]] = dsum[j, far[d]]
            landing = y1b[d].at[near[d]]
            wire.landed(ys1[d], landing, ydev[-d])
            y1b[d][near[d]] = total_of([landing, dsum.at[j, near[d]]])
            wire.start(ys2[d], y1b[d], y2b[d], ydev[d])

    b_step(2)

    for d in (1, -1):
        wire.landed(ys2[d], y2b[d], ydev[-d])
    agg = total_of([dsum.at[0], y2p, y2m])
    layer[...] = lax.dot_general(
        agg, w[...], (((0,), (0,)), ((), ())), preferred_element_type=F32).astype(BF)

    for u in (1, 0):
        for d in (1, -1):
            wire.landed(bs[d, 3, u], bb[d].at[3, u], zdev[-d])
        e[u] = total_of([bt_at(0, u), bp.at[3, u], bm.at[3, u]])
        if u == 1:
            wire.start(yls, e.at[1], ylr, ylo)
    wire.landed(yls, ylr, ylo)
    feat[...] = total_of([e.at[0], ylr])

    others = gall.at[pl.ds(1, N_COL - 1)]
    pltpu.make_async_copy(others, others, grecv.at[2]).wait()
    for q in range(N_COL):
        a, h = q // 2, q % 2
        chunk = gall[(col - q + N_COL) % N_COL].astype(F32) * scale
        wgrad[a * 16:(a + 1) * 16, h * TILE:(h + 1) * TILE] = chunk
    pltpu.make_async_copy(g_in, g_in, gsend.at[0]).wait()
    pltpu.make_async_copy(g_row, g_row, gsend.at[1]).wait()
    pltpu.make_async_copy(others, others, gsend.at[2]).wait()
    wire.drain()


def reduce(pt, bt, g, w, scale):
    vmem = pl.BlockSpec(memory_space=pltpu.VMEM)
    return pl.pallas_call(
        functools.partial(reduce_kernel, scale),
        out_shape=(
            jax.ShapeDtypeStruct((TILE, F), BF),
            jax.ShapeDtypeStruct((TC, F // N_ROW, TILE), BF),
            jax.ShapeDtypeStruct((F, F), F32),
        ),
        in_specs=[vmem] * 4,
        out_specs=(vmem, vmem, vmem),
        scratch_shapes=[
            pltpu.VMEM((N_COL, 16, TILE), BF),
            pltpu.VMEM((NYH, NX, F, TILE), BF),
            pltpu.VMEM((NYH, NX, F, TILE), BF),
            pltpu.VMEM((NYH, F, TILE), BF),
            pltpu.VMEM((NYH, F, TILE), BF),
            pltpu.VMEM((NYH, F, TILE), BF),
            pltpu.VMEM((NYH, F, TILE), BF),
            pltpu.VMEM((NYH, F, TILE), BF),
            pltpu.VMEM((F, TILE), BF),
            pltpu.VMEM((F, TILE), BF),
            pltpu.VMEM((F, TILE), BF),
            pltpu.VMEM((F, TILE), BF),
            pltpu.VMEM((4, NYL, TC, F // N_ROW, TILE), BF),
            pltpu.VMEM((4, NYL, TC, F // N_ROW, TILE), BF),
            pltpu.VMEM((NYL, TC, F // N_ROW, TILE), BF),
            pltpu.VMEM((TC, F // N_ROW, TILE), BF),
            pltpu.VMEM((N_COL - 1, 16, TILE), BF),
            pltpu.VMEM((16, TILE), BF),
            pltpu.VMEM((N_ROW - 1, 16, TILE), BF),
            pltpu.VMEM((16, TILE), BF),
            pltpu.SemaphoreType.DMA((N_REDUCE,)),
            pltpu.SemaphoreType.DMA((N_REDUCE,)),
            pltpu.SemaphoreType.DMA((3,)),
            pltpu.SemaphoreType.DMA((3,)),
        ],
        compiler_params=pltpu.CompilerParams(
            collective_id=1, has_side_effects=True, vmem_limit_bytes=32 << 20),
        name="reduce",
    )(pt, bt, g, w)


def local(x_feat, weight, tile_vals, tile_row, tile_col, tile_live, d_out):
    nodes = d_out.shape[0] * N_COL * N_ROW
    xt = x_feat.reshape(TC, TILE, F // N_ROW).transpose(0, 2, 1)
    xg, dg = gather(xt, d_out)
    pt, bt, g = cell(tile_row[0, 0], tile_col[0, 0], tile_live[0, 0], tile_vals[0, 0], xg, dg, weight)
    scale = 1.0 / math.sqrt(nodes)
    layer, feat, wgrad = reduce(pt.reshape(NYH, NX, NK, F, TILE), bt, g, weight, scale)
    feat = feat.transpose(0, 2, 1).reshape(TC * TILE, F // N_ROW)
    return layer, wgrad, feat


def solution(mesh):
    placed = (
        P("col", "row"),
        P(),
        P("row", "col", None, None, None),
        P("row", "col", None),
        P("row", "col", None),
        P("row", "col", None),
        P(("row", "col"), None),
    )
    return jax.shard_map(
        local,
        mesh=mesh,
        in_specs=placed,
        out_specs=(P(("row", "col"), None), P(), P("col", "row")),
        check_vma=False,
    )
```

```python
import functools
import math

import jax
import jax.numpy as jnp
from jax import lax
from jax.experimental import pallas as pl
from jax.experimental.pallas import tpu as pltpu
from jax.sharding import PartitionSpec as P

TILE = 128
F = 256
NZ, NYL = 8, 2
NYH, NX, NK = 4, 4, 2
N_ROW, N_COL = NZ * NYL, NYH * NX * NK
SLOTS = 96
TR, TC = 32, 16
BF = jnp.bfloat16
F32 = jnp.float32
MESH = pl.DeviceIdType.MESH


def place():
    row, col = lax.axis_index("row"), lax.axis_index("col")
    return row // NYL, row % NYL, col // (NX * NK), (col // NK) % NX, col % NK


class Wire:
    def __init__(self, send, recv):
        self.send, self.recv, self.used, self.started = send, recv, 0, []

    def slot(self):
        self.used += 1
        return self.used - 1

    def start(self, slot, src, dst, device):
        copy = pltpu.make_async_remote_copy(
            src_ref=src, dst_ref=dst, send_sem=self.send.at[slot], recv_sem=self.recv.at[slot],
            device_id=device, device_id_type=MESH)
        copy.start()
        self.started.append(copy)

    def landed(self, slot, dst, device):
        pltpu.make_async_remote_copy(
            src_ref=dst, dst_ref=dst, send_sem=self.send.at[slot], recv_sem=self.recv.at[slot],
            device_id=device, device_id_type=MESH).wait_recv()

    def drain(self):
        for copy in self.started:
            copy.wait_send()


def devices_around():
    z, yl, yh, x, k = place()

    def at(dz=0, dyl=0, dyh=0, dx=0, dk=0):
        row = ((z + dz) % NZ) * NYL + (yl + dyl) % NYL
        col = (((yh + dyh) % NYH) * NX + (x + dx) % NX) * NK + (k + dk) % NK
        return row, col

    return at


N_LINK = 1 + 16 + 3 + 12 + 16 + 4 + 12 + 3 + 16 + 1
UNROLL = 8
RUN = 32
NT = (((1,), (1,)), ((), ()))
TN = (((0,), (0,)), ((), ()))


def total_of(refs):
    out = refs[0][...].astype(F32)
    for ref in refs[1:]:
        out += ref[...].astype(F32)
    return out.astype(BF)


def sorted_rows(key, other, rows):
    shape = (TILE, TILE)
    lane = lax.broadcasted_iota(jnp.int32, shape, 1)
    down = lax.broadcasted_iota(jnp.int32, shape, 0)
    keys = jnp.broadcast_to(key, shape)
    mine = keys * TILE + lane
    theirs = mine.T
    rank = jnp.sum((mine < theirs).astype(jnp.int32), axis=1, keepdims=True)
    hot = rank == lane
    key_down = keys.T
    other_down = jnp.broadcast_to(other, shape).T
    for i, value in enumerate((down, other_down, key_down)):
        rows[i:i + 1, :] = jnp.sum(jnp.where(hot, value, 0), axis=0, keepdims=True)
    rows[3:4, :] = jnp.sum((key_down <= lane).astype(jnp.int32), axis=0, keepdims=True)


def layer_kernel(scale, x_in, w_in, vals_in, trow_in, tcol_in, live_in, d_in, layer, feat, wgrad,
                 wl, w, vals, idx, keys, meta_v, meta, xl, dl, xg, dg, runs, pt, bt,
                 core_in, c, xin, dsum, yin, b1, b2, b3, b4, bmid, e, ylr, g, g_in, g_part,
                 loads, send, recv, gsend, grecv):
    z, yl, yh, x, k = place()
    at = devices_around()
    row, col = at()
    wire = Wire(send, recv)
    zdev = {1: at(dz=1), -1: at(dz=-1)}
    sib, ylo = at(dk=1), at(dyl=1)
    barrier = pltpu.get_barrier_semaphore()

    m, n = col % (NX * NK), yh * NYL + yl

    def plane_x(o):
        return row, yh * (NX * NK) + (m + o) % 8

    def plane_y(o):
        there = (n + o) % 8
        return z * NYL + there % NYL, there // NYL * (NX * NK) + m

    def plane_z(o):
        return (z + o) % NZ * NYL + yl, col

    groups = (plane_x, plane_y, plane_z)
    for group in groups:
        for o in range(1, 8):
            pl.semaphore_signal(barrier, inc=1, device_id=group(o), device_id_type=MESH)

    load = [
        pltpu.make_async_copy(src, dst, loads.at[i])
        for i, (src, dst) in enumerate((
            (x_in, xl), (d_in, dl),
            (trow_in.at[0], idx.at[0]), (tcol_in.at[0], idx.at[1]), (live_in.at[0], idx.at[2]),
            (w_in, wl), (vals_in.at[0, 0], vals)))
    ]
    for copy in load:
        copy.start()
    load[0].wait()
    for t in range(TC):
        xg[1, 0, t] = xl[:, t * TILE:(t + 1) * TILE]
    load[1].wait()
    dg[col] = dl[...].astype(F32).T.astype(BF)
    pl.semaphore_wait(barrier, 7 * len(groups))

    ys = wire.slot()
    zs = {(d, s, u): wire.slot() for d in (1, -1) for s in (1, 2, 3, 4) for u in (0, 1)}
    half = {1: pl.ds(0, TC // 2), -1: pl.ds(TC // 2, TC // 2)}

    def xpart(dz, u, d, s):
        ref = xg.at[(dz + 1) % NZ, u]
        return ref.at[half[d]] if s == 4 else ref

    def z_send(d, s, u):
        hop = s if s < 3 else s - 2
        back = 0 if s < 3 else -2 * d
        wire.start(zs[d, s, u], xpart(back, u, d, s), xpart(-d * s, u, d, s), at(dz=hop * d))

    def z_landed(d, s, u):
        hop = s if s < 3 else s - 2
        wire.landed(zs[d, s, u], xpart(-d * s, u, d, s), at(dz=-hop * d))

    def z_first(u):
        for s in (2, 1):
            for d in (1, -1):
                z_send(d, s, u)

    def z_second(u):
        for d in (1, -1):
            z_landed(d, 2, u)
            for s in (3, 4):
                z_send(d, s, u)

    def z_third():
        for s in (1, 3, 4):
            for u in (0, 1):
                for d in (1, -1):
                    z_landed(d, s, u)

    def piece(j, dx=0, dk=0):
        return dg.at[at(dyh=j, dx=dx, dk=dk)[1]]

    dys = {o: wire.slot() for o in (1, 3, 2)}
    dxs = {(j, o): wire.slot() for j in range(4) for o in (1, 3, 2)}
    dks = {(j, dx): wire.slot() for j in range(4) for dx in range(4)}

    def d_to_x(j):
        for o in (1, 3, 2):
            wire.start(dxs[j, o], piece(j), piece(j), at(dx=o))
        wire.start(dks[j, 0], piece(j), piece(j), sib)

    def d_x_landed(j):
        for o in (1, 3, 2):
            part = piece(j, -o)
            wire.landed(dxs[j, o], part, at(dx=-o))
            wire.start(dks[j, -o % 4], part, part, sib)

    mine = xg.at[1, 0]
    z_first(0)
    wire.start(ys, mine, xg.at[1, 1], ylo)
    for o in (1, 3, 2):
        wire.start(dys[o], piece(0), piece(0), at(dyh=o))
    d_to_x(0)

    for copy in load[2:5]:
        copy.wait()
    keys[...] = jnp.full(keys.shape, TILE - 1, jnp.int32)
    for i in range(3):
        keys[i:i + 1, 0:SLOTS] = idx[i]
    alive = keys[2:3, :] > 0
    sorted_rows(jnp.where(alive, keys[0:1, :], TR), keys[1:2, :], meta_v.at[0:4])
    wire.landed(ys, xg.at[1, 1], ylo)
    z_first(1)
    sorted_rows(jnp.where(alive, keys[1:2, :], TC), keys[0:1, :], meta_v.at[4:8])
    to_scalars = pltpu.make_async_copy(meta_v, meta, loads.at[0])
    to_scalars.start()

    z_second(0)
    for o in (1, 3):
        wire.landed(dys[o], piece(-o), at(dyh=-o))
        d_to_x(-o % 4)
    z_second(1)
    wire.landed(dys[2], piece(2), at(dyh=2))
    d_to_x(2)
    d_x_landed(0)
    load[5].wait()
    for i in range(NZ):
        for u in (0, 1):
            b = (i * NYL + u) * (F // N_ROW)
            w[b:b + F // N_ROW, :] = wl[at(dz=i - 1, dyl=u)[0]]
    to_scalars.wait()
    load[6].wait()

    def run(base, source, contract):
        def step(i, acc):
            for v in range(RUN):
                s = i * RUN + v
                slot, other = meta[base, s], meta[base + 1, s]
                same = jnp.logical_and(s > 0, meta[base + 2, s] == meta[base + 2, jnp.maximum(s - 1, 0)])
                prod = lax.dot_general(source(other), vals[slot], contract, preferred_element_type=F32)
                acc = jnp.where(same, acc + prod, prod)
                runs[s] = acc.astype(BF)
            return acc
        lax.fori_loop(0, SLOTS // RUN, step, jnp.zeros((F, TILE), F32))

    def last_of(base, t):
        count = meta[base + 3, t]
        before = jnp.where(t > 0, meta[base + 3, jnp.maximum(t - 1, 0)], 0)
        value = runs[jnp.maximum(count - 1, 0)]
        return jnp.where(count > before, value, jnp.zeros_like(value))

    z_third()
    run(0, lambda i: xg[:, :, i].reshape(F, TILE), NT)

    order = (2, 1, 3, 0)
    near = (1, 3, 2)

    def yy(j):
        return (yh + j) % NYH

    cs = {j: wire.slot() for j in order}
    pxs = {(j, o): wire.slot() for j in order for o in near}
    pys = {o: wire.slot() for o in near}

    def fill(core):
        def one(i, carry):
            for v in range(NX):
                pt[i, v, core] = last_of(0, (i * NX + v) * NK + core)
            return carry
        return one

    lax.fori_loop(0, NYH, fill(1 - k), 0)
    for j in order:
        wire.start(cs[j], pt.at[yy(j), :, 1 - k], core_in.at[yy(j)], sib)

    for j in (3, 1, 2):
        d_x_landed(j)
    lax.fori_loop(0, NYH, fill(k), 0)

    b1s, b2s, b3s, b4s = ({(d, u): wire.slot() for d in (1, -1) for u in (0, 1)} for _ in range(4))
    side = {1: 0, -1: 1}
    yls = wire.slot()

    def bt_at(dz, u):
        return bt.at[(dz + 1) % NZ, u]

    def b_start():
        for u in (1, 0):
            for d in (1, -1):
                wire.start(b3s[d, u], bt_at(3 * d, u), b3.at[side[d], u], zdev[d])
                wire.start(b4s[d, u], bt_at(4, u).at[half[d]], b4.at[side[d], u], at(dz=2 * d))
        for u in (1, 0):
            for d in (1, -1):
                wire.start(b1s[d, u], bt_at(d, u), b1.at[side[d], u], zdev[d])

    def b_middle():
        for u in (1, 0):
            for d in (1, -1):
                wire.landed(b3s[d, u], b3.at[side[d], u], zdev[-d])
                wire.landed(b4s[d, u], b4.at[side[d], u], at(dz=-2 * d))
                mid, own = bmid.at[side[d], u], bt_at(2 * d, u)
                mid[half[-d]] = total_of([own.at[half[-d]], b3.at[side[d], u, half[-d]]])
                mid[half[d]] = total_of([own.at[half[d]], b3.at[side[d], u, half[d]], b4.at[side[d], u]])
                wire.start(b2s[d, u], mid, b2.at[side[d], u], at(dz=2 * d))

    for j in order:
        wire.landed(cs[j], core_in.at[yy(j)], sib)

        def add(i, carry):
            c[yy(j), i] = total_of([pt.at[yy(j), i, k], core_in.at[yy(j), i]])
            return carry

        lax.fori_loop(0, NX, add, 0)
        for o in near:
            wire.start(pxs[j, o], c.at[yy(j), (x + o) % NX], xin.at[o - 1, j], at(dx=o))

    def spread(i, carry):
        for v in range(UNROLL):
            t = i * UNROLL + v
            term = jnp.dot(w[...], last_of(4, t), preferred_element_type=F32)
            bt[:, :, t] = term.astype(BF).reshape(NZ, NYL, F // N_ROW, TILE)
        return carry

    for j in (0, 3, 1, 2):
        for dx in range(4):
            wire.landed(dks[j, dx], piece(j, dx, 1), sib)

    run(4, lambda i: dg[i], (((1,), (0,)), ((), ())))
    lax.fori_loop(0, TC // UNROLL, spread, 0)
    b_start()

    def grad_term(i, total):
        for v in range(UNROLL):
            total += lax.dot_general(
                pt[i, v // NK, v % NK], dg[i * UNROLL + v], NT, preferred_element_type=F32)
        return total

    total = lax.fori_loop(0, TR // UNROLL, grad_term, jnp.zeros((F, F), F32)).astype(BF)
    for i in range(NZ):
        for u in (0, 1):
            b, a = (i * NYL + u) * 16, at(dz=i - 1, dyl=u)[0]
            for h in (0, 1):
                g[2 * a + h] = total[b:b + 16, h * TILE:(h + 1) * TILE]

    def g_exchange(stage, group, source):
        for o in range(1, 8):
            pltpu.make_async_remote_copy(
                src_ref=source(o), dst_ref=g_in.at[stage, o - 1],
                send_sem=gsend.at[stage], recv_sem=grecv.at[stage],
                device_id=group(o), device_id_type=MESH).start()

    def g_landed(stage):
        landing = g_in.at[stage, pl.ds(0, 7)]
        pltpu.make_async_copy(landing, landing, grecv.at[stage]).wait()

    def g_add(stage, own):
        g_landed(stage)
        g_part[stage] = (jnp.sum(g_in[stage, 0:7].astype(F32), axis=0) + own[...].astype(F32)).astype(BF)

    g_exchange(0, plane_x, lambda o: g.at[pl.ds((m + o) % 8 * 4, 4)])

    def p_x_landed(j):
        for o in near:
            wire.landed(pxs[j, o], xin.at[o - 1, j], at(dx=-o))
        dsum[j] = total_of([c.at[yy(j), x], xin.at[0, j], xin.at[1, j], xin.at[2, j]])
        if j:
            wire.start(pys[j], dsum.at[j], yin.at[j - 1], at(dyh=j))

    p_x_landed(2)
    b_middle()
    p_x_landed(1)

    g_add(0, g.at[pl.ds(m * 4, 4)])
    g_exchange(1, plane_y, lambda o: g_part.at[0])

    p_x_landed(3)

    g_add(1, g_part.at[0])
    g_exchange(2, plane_z, lambda o: g_part.at[1])

    p_x_landed(0)

    g_add(2, g_part.at[1])
    g_exchange(3, plane_x, lambda o: g_part.at[2])

    for u in (1, 0):
        for d in (1, -1):
            wire.landed(b1s[d, u], b1.at[side[d], u], zdev[-d])
            wire.landed(b2s[d, u], b2.at[side[d], u], at(dz=-2 * d))
        e[u] = total_of([bt_at(0, u), b1.at[0, u], b1.at[1, u], b2.at[0, u], b2.at[1, u]])
        if u == 1:
            wire.start(yls, e.at[1], ylr, ylo)

    for o in near:
        wire.landed(pys[o], yin.at[o - 1], at(dyh=-o))
    agg = total_of([dsum.at[0], yin.at[0], yin.at[1], yin.at[2]])
    layer[...] = lax.dot_general(agg, w[...], TN, preferred_element_type=F32).astype(BF)

    g_landed(3)
    g_in[3, 7] = g_part[2]
    for q in range(N_COL):
        a, h = q // 2, q % 2
        chunk = g_in[3, (m - q // 4 + 7) % 8, q % 4].astype(F32) * scale
        wgrad[a * 16:(a + 1) * 16, h * TILE:(h + 1) * TILE] = chunk

    wire.landed(yls, ylr, ylo)
    mine = total_of([e.at[0], ylr])
    for t in range(TC):
        feat[:, t * TILE:(t + 1) * TILE] = mine[t]

    for stage in range(4):
        sent = g_in.at[stage, pl.ds(0, 7)]
        pltpu.make_async_copy(sent, sent, gsend.at[stage]).wait()
    wire.drain()


def layer_call(xt, w, vals, trow, tcol, live, d_out, scale):
    vmem = pl.BlockSpec(memory_space=pltpu.VMEM)
    here = pl.BlockSpec(memory_space=pltpu.HBM)
    fr = F // N_ROW
    ints = jnp.int32
    return pl.pallas_call(
        functools.partial(layer_kernel, scale),
        out_shape=(
            jax.ShapeDtypeStruct((TILE, F), BF),
            jax.ShapeDtypeStruct((fr, TC * TILE), BF),
            jax.ShapeDtypeStruct((F, F), F32),
        ),
        in_specs=[here] * 7,
        out_specs=(vmem, vmem, vmem),
        scratch_shapes=[
            pltpu.VMEM((N_ROW, F // N_ROW, F), BF),
            pltpu.VMEM((F, F), BF),
            pltpu.VMEM((SLOTS, TILE, TILE), BF),
            pltpu.VMEM((3, 1, SLOTS), ints),
            pltpu.VMEM((8, TILE), ints),
            pltpu.VMEM((8, TILE), ints),
            pltpu.SMEM((8, TILE), ints),
            pltpu.VMEM((fr, TC * TILE), BF),
            pltpu.VMEM((TILE, F), BF),
            pltpu.VMEM((NZ, NYL, TC, fr, TILE), BF),
            pltpu.VMEM((N_COL, F, TILE), BF),
            pltpu.VMEM((SLOTS, F, TILE), BF),
            pltpu.VMEM((NYH, NX, NK, F, TILE), BF),
            pltpu.VMEM((NZ, NYL, TC, fr, TILE), BF),
            pltpu.VMEM((NYH, NX, F, TILE), BF),
            pltpu.VMEM((NYH, NX, F, TILE), BF),
            pltpu.VMEM((NX - 1, NYH, F, TILE), BF),
            pltpu.VMEM((NYH, F, TILE), BF),
            pltpu.VMEM((NYH - 1, F, TILE), BF),
            pltpu.VMEM((2, NYL, TC, fr, TILE), BF),
            pltpu.VMEM((2, NYL, TC, fr, TILE), BF),
            pltpu.VMEM((2, NYL, TC, fr, TILE), BF),
            pltpu.VMEM((2, NYL, TC // 2, fr, TILE), BF),
            pltpu.VMEM((2, NYL, TC, fr, TILE), BF),
            pltpu.VMEM((NYL, TC, fr, TILE), BF),
            pltpu.VMEM((TC, fr, TILE), BF),
            pltpu.VMEM((N_COL, 16, TILE), BF),
            pltpu.VMEM((4, 8, 4, 16, TILE), BF),
            pltpu.VMEM((3, 4, 16, TILE), BF),
            pltpu.SemaphoreType.DMA((7,)),
            pltpu.SemaphoreType.DMA((N_LINK,)),
            pltpu.SemaphoreType.DMA((N_LINK,)),
            pltpu.SemaphoreType.DMA((4,)),
            pltpu.SemaphoreType.DMA((4,)),
        ],
        compiler_params=pltpu.CompilerParams(
            collective_id=0, has_side_effects=True, vmem_limit_bytes=56 << 20),
        name="graph_layer",
    )(xt, w.reshape(N_ROW, fr, F), vals, trow, tcol, live, d_out)


def local(x_feat, weight, tile_vals, tile_row, tile_col, tile_live, d_out):
    nodes = d_out.shape[0] * N_COL * N_ROW
    layer, feat, wgrad = layer_call(
        x_feat.T, weight, tile_vals, tile_row, tile_col, tile_live, d_out, 1.0 / math.sqrt(nodes))
    return layer, wgrad, feat.T


def solution(mesh):
    placed = (
        P("col", "row"),
        P(),
        P("row", "col", None, None, None),
        P("row", "col", None),
        P("row", "col", None),
        P("row", "col", None),
        P(("row", "col"), None),
    )
    return jax.shard_map(
        local,
        mesh=mesh,
        in_specs=placed,
        out_specs=(P(("row", "col"), None), P(), P("col", "row")),
        check_vma=False,
    )
```

```python
import functools
import math

import jax
import jax.numpy as jnp
from jax import lax
from jax.experimental import pallas as pl
from jax.experimental.pallas import tpu as pltpu
from jax.sharding import PartitionSpec as P

TILE = 128
F = 256
NZ, NYL = 8, 2
NYH, NX, NK = 4, 4, 2
N_ROW, N_COL = NZ * NYL, NYH * NX * NK
SLOTS = 96
TR, TC = 32, 16
BF = jnp.bfloat16
F32 = jnp.float32
MESH = pl.DeviceIdType.MESH


def place():
    row, col = lax.axis_index("row"), lax.axis_index("col")
    return row // NYL, row % NYL, col // (NX * NK), (col // NK) % NX, col % NK


class Wire:
    def __init__(self, send, recv):
        self.send, self.recv, self.used, self.started = send, recv, 0, []

    def slot(self):
        self.used += 1
        return self.used - 1

    def start(self, slot, src, dst, device):
        copy = pltpu.make_async_remote_copy(
            src_ref=src, dst_ref=dst, send_sem=self.send.at[slot], recv_sem=self.recv.at[slot],
            device_id=device, device_id_type=MESH)
        copy.start()
        self.started.append(copy)

    def landed(self, slot, dst, device):
        pltpu.make_async_remote_copy(
            src_ref=dst, dst_ref=dst, send_sem=self.send.at[slot], recv_sem=self.recv.at[slot],
            device_id=device, device_id_type=MESH).wait_recv()

    def drain(self):
        for copy in self.started:
            copy.wait_send()


def devices_around():
    z, yl, yh, x, k = place()

    def at(dz=0, dyl=0, dyh=0, dx=0, dk=0):
        row = ((z + dz) % NZ) * NYL + (yl + dyl) % NYL
        col = (((yh + dyh) % NYH) * NX + (x + dx) % NX) * NK + (k + dk) % NK
        return row, col

    return at


N_LINK = 1 + 16 + 3 + 12 + 16 + 4 + 12 + 3 + 16 + 1
UNROLL = 8
RUN = 32
NT = (((1,), (1,)), ((), ()))
TN = (((0,), (0,)), ((), ()))


def total_of(refs):
    out = refs[0][...].astype(F32)
    for ref in refs[1:]:
        out += ref[...].astype(F32)
    return out.astype(BF)


def sorted_rows(key, other, rows):
    shape = (TILE, TILE)
    lane = lax.broadcasted_iota(jnp.int32, shape, 1)
    down = lax.broadcasted_iota(jnp.int32, shape, 0)
    keys = jnp.broadcast_to(key, shape)
    mine = keys * TILE + lane
    theirs = mine.T
    rank = jnp.sum((mine < theirs).astype(jnp.int32), axis=1, keepdims=True)
    hot = rank == lane
    key_down = keys.T
    other_down = jnp.broadcast_to(other, shape).T
    for i, value in enumerate((down, other_down, key_down)):
        rows[i:i + 1, :] = jnp.sum(jnp.where(hot, value, 0), axis=0, keepdims=True)
    rows[3:4, :] = jnp.sum((key_down <= lane).astype(jnp.int32), axis=0, keepdims=True)


def layer_kernel(scale, x_in, w_in, vals_in, trow_in, tcol_in, live_in, d_in, layer, feat, wgrad,
                 wl, w, vals, idx, keys, meta_v, meta, xl, dl, xg, dg, runs, pt, bt,
                 core_in, c, xin, dsum, yin, b1, b2, b3, b4, bmid, e, ylr, g, g_in, g_part,
                 loads, send, recv, gsend, grecv):
    z, yl, yh, x, k = place()
    at = devices_around()
    row, col = at()
    wire = Wire(send, recv)
    zdev = {1: at(dz=1), -1: at(dz=-1)}
    sib, ylo = at(dk=1), at(dyl=1)
    barrier = pltpu.get_barrier_semaphore()

    m, n = col % (NX * NK), yh * NYL + yl

    def plane_x(o):
        return row, yh * (NX * NK) + (m + o) % 8

    def plane_y(o):
        there = (n + o) % 8
        return z * NYL + there % NYL, there // NYL * (NX * NK) + m

    def plane_z(o):
        return (z + o) % NZ * NYL + yl, col

    groups = (plane_x, plane_y, plane_z)
    for group in groups:
        for o in range(1, 8):
            pl.semaphore_signal(barrier, inc=1, device_id=group(o), device_id_type=MESH)

    load = [
        pltpu.make_async_copy(src, dst, loads.at[i])
        for i, (src, dst) in enumerate((
            (x_in, xl), (d_in, dl),
            (trow_in.at[0], idx.at[0]), (tcol_in.at[0], idx.at[1]), (live_in.at[0], idx.at[2]),
            (w_in, wl), (vals_in.at[0, 0], vals)))
    ]
    for copy in load:
        copy.start()
    load[0].wait()
    for t in range(TC):
        xg[1, 0, t] = xl[:, t * TILE:(t + 1) * TILE]
    load[1].wait()
    dg[col] = dl[...].astype(F32).T.astype(BF)
    pl.semaphore_wait(barrier, 7 * len(groups))

    ys = wire.slot()
    zs = {(d, s, u): wire.slot() for d in (1, -1) for s in (1, 2, 3, 4) for u in (0, 1)}
    half = {1: pl.ds(0, TC // 2), -1: pl.ds(TC // 2, TC // 2)}

    def xpart(dz, u, d, s):
        ref = xg.at[(dz + 1) % NZ, u]
        return ref.at[half[d]] if s == 4 else ref

    def z_send(d, s, u):
        hop = s if s < 3 else s - 2
        back = 0 if s < 3 else -2 * d
        wire.start(zs[d, s, u], xpart(back, u, d, s), xpart(-d * s, u, d, s), at(dz=hop * d))

    def z_landed(d, s, u):
        hop = s if s < 3 else s - 2
        wire.landed(zs[d, s, u], xpart(-d * s, u, d, s), at(dz=-hop * d))

    def z_first(u):
        for s in (2, 1):
            for d in (1, -1):
                z_send(d, s, u)

    def z_second(u):
        for d in (1, -1):
            z_landed(d, 2, u)
            for s in (3, 4):
                z_send(d, s, u)

    def z_third():
        for s in (1, 3, 4):
            for u in (0, 1):
                for d in (1, -1):
                    z_landed(d, s, u)

    def piece(j, dx=0, dk=0):
        return dg.at[at(dyh=j, dx=dx, dk=dk)[1]]

    dys = {o: wire.slot() for o in (1, 3, 2)}
    dxs = {(j, o): wire.slot() for j in range(4) for o in (1, 3, 2)}
    dks = {(j, dx): wire.slot() for j in range(4) for dx in range(4)}

    def d_to_x(j):
        for o in (1, 3, 2):
            wire.start(dxs[j, o], piece(j), piece(j), at(dx=o))
        wire.start(dks[j, 0], piece(j), piece(j), sib)

    def d_x_landed(j):
        for o in (1, 3, 2):
            part = piece(j, -o)
            wire.landed(dxs[j, o], part, at(dx=-o))
            wire.start(dks[j, -o % 4], part, part, sib)

    mine = xg.at[1, 0]
    z_first(0)
    wire.start(ys, mine, xg.at[1, 1], ylo)
    for o in (1, 3, 2):
        wire.start(dys[o], piece(0), piece(0), at(dyh=o))
    d_to_x(0)

    for copy in load[2:5]:
        copy.wait()
    keys[...] = jnp.full(keys.shape, TILE - 1, jnp.int32)
    for i in range(3):
        keys[i:i + 1, 0:SLOTS] = idx[i]
    alive = keys[2:3, :] > 0
    sorted_rows(jnp.where(alive, keys[0:1, :], TR), keys[1:2, :], meta_v.at[0:4])
    wire.landed(ys, xg.at[1, 1], ylo)
    z_first(1)
    sorted_rows(jnp.where(alive, keys[1:2, :], TC), keys[0:1, :], meta_v.at[4:8])
    to_scalars = pltpu.make_async_copy(meta_v, meta, loads.at[0])
    to_scalars.start()

    z_second(0)
    for o in (1, 3):
        wire.landed(dys[o], piece(-o), at(dyh=-o))
        d_to_x(-o % 4)
    z_second(1)
    wire.landed(dys[2], piece(2), at(dyh=2))
    d_to_x(2)
    d_x_landed(0)
    load[5].wait()
    for i in range(NZ):
        for u in (0, 1):
            b = (i * NYL + u) * (F // N_ROW)
            w[b:b + F // N_ROW, :] = wl[at(dz=i - 1, dyl=u)[0]]
    to_scalars.wait()
    load[6].wait()

    def run(base, source, contract, begin=0, end=SLOTS // RUN, acc=None):
        def step(i, acc):
            for v in range(RUN):
                s = i * RUN + v
                slot, other = meta[base, s], meta[base + 1, s]
                same = jnp.logical_and(s > 0, meta[base + 2, s] == meta[base + 2, jnp.maximum(s - 1, 0)])
                prod = lax.dot_general(source(other), vals[slot], contract, preferred_element_type=F32)
                acc = jnp.where(same, acc + prod, prod)
                runs[s] = acc.astype(BF)
            return acc
        acc = jnp.zeros((F, TILE), F32) if acc is None else acc
        return lax.fori_loop(begin, end, step, acc)

    def last_of(base, t):
        count = meta[base + 3, t]
        before = jnp.where(t > 0, meta[base + 3, jnp.maximum(t - 1, 0)], 0)
        value = runs[jnp.maximum(count - 1, 0)]
        return jnp.where(count > before, value, jnp.zeros_like(value))

    z_third()
    run(0, lambda i: xg[:, :, i].reshape(F, TILE), NT)

    order = (2, 1, 3, 0)
    near = (1, 3, 2)

    def yy(j):
        return (yh + j) % NYH

    cs = {j: wire.slot() for j in order}
    pxs = {(j, o): wire.slot() for j in order for o in near}
    pys = {o: wire.slot() for o in near}

    def fill(core):
        def one(i, carry):
            for v in range(NX):
                pt[i, v, core] = last_of(0, (i * NX + v) * NK + core)
            return carry
        return one

    lax.fori_loop(0, NYH, fill(1 - k), 0)
    for j in order:
        wire.start(cs[j], pt.at[yy(j), :, 1 - k], core_in.at[yy(j)], sib)

    for j in (3, 1, 2):
        d_x_landed(j)
    lax.fori_loop(0, NYH, fill(k), 0)

    b1s, b2s, b3s, b4s = ({(d, u): wire.slot() for d in (1, -1) for u in (0, 1)} for _ in range(4))
    side = {1: 0, -1: 1}
    yls = wire.slot()

    def bt_at(dz, u):
        return bt.at[(dz + 1) % NZ, u]

    def b_start():
        for u in (1, 0):
            for d in (1, -1):
                wire.start(b3s[d, u], bt_at(3 * d, u), b3.at[side[d], u], zdev[d])
                wire.start(b4s[d, u], bt_at(4, u).at[half[d]], b4.at[side[d], u], at(dz=2 * d))
        for u in (1, 0):
            for d in (1, -1):
                wire.start(b1s[d, u], bt_at(d, u), b1.at[side[d], u], zdev[d])

    def b_middle():
        for u in (1, 0):
            for d in (1, -1):
                wire.landed(b3s[d, u], b3.at[side[d], u], zdev[-d])
                wire.landed(b4s[d, u], b4.at[side[d], u], at(dz=-2 * d))
                mid, own = bmid.at[side[d], u], bt_at(2 * d, u)
                mid[half[-d]] = total_of([own.at[half[-d]], b3.at[side[d], u, half[-d]]])
                mid[half[d]] = total_of([own.at[half[d]], b3.at[side[d], u, half[d]], b4.at[side[d], u]])
                wire.start(b2s[d, u], mid, b2.at[side[d], u], at(dz=2 * d))

    def spread(i, carry):
        for v in range(UNROLL):
            t = i * UNROLL + v
            term = jnp.dot(w[...], last_of(4, t), preferred_element_type=F32)
            bt[:, :, t] = term.astype(BF).reshape(NZ, NYL, F // N_ROW, TILE)
        return carry

    for j in order:
        wire.landed(cs[j], core_in.at[yy(j)], sib)

        def add(i, carry):
            c[yy(j), i] = total_of([pt.at[yy(j), i, k], core_in.at[yy(j), i]])
            return carry

        lax.fori_loop(0, NX, add, 0)

    def grad_term(i, total):
        for v in range(NX):
            total += lax.dot_general(
                c[i, v], dg[(i * NX + v) * NK + k], NT, preferred_element_type=F32)
        return total

    total = lax.fori_loop(0, NYH, grad_term, jnp.zeros((F, F), F32)).astype(BF)
    for i in range(NZ):
        for u in (0, 1):
            b, a = (i * NYL + u) * 16, at(dz=i - 1, dyl=u)[0]
            for h in (0, 1):
                g[2 * a + h] = total[b:b + 16, h * TILE:(h + 1) * TILE]

    def g_exchange(stage, group, source):
        for o in range(1, 8):
            pltpu.make_async_remote_copy(
                src_ref=source(o), dst_ref=g_in.at[stage, o - 1],
                send_sem=gsend.at[stage], recv_sem=grecv.at[stage],
                device_id=group(o), device_id_type=MESH).start()

    def g_landed(stage):
        landing = g_in.at[stage, pl.ds(0, 7)]
        pltpu.make_async_copy(landing, landing, grecv.at[stage]).wait()

    def g_add(stage, own):
        g_landed(stage)
        g_part[stage] = (jnp.sum(g_in[stage, 0:7].astype(F32), axis=0) + own[...].astype(F32)).astype(BF)

    g_exchange(0, plane_x, lambda o: g.at[pl.ds((m + o) % 8 * 4, 4)])

    for j in order:
        for o in near:
            wire.start(pxs[j, o], c.at[yy(j), (x + o) % NX], xin.at[o - 1, j], at(dx=o))

    for j in (0, 3, 1, 2):
        for dx in range(4):
            wire.landed(dks[j, dx], piece(j, dx, 1), sib)

    part = run(4, lambda i: dg[i], (((1,), (0,)), ((), ())), 0, 1)
    g_add(0, g.at[pl.ds(m * 4, 4)])
    g_exchange(1, plane_z, lambda o: g_part.at[0])
    run(4, lambda i: dg[i], (((1,), (0,)), ((), ())), 1, SLOTS // RUN, part)
    lax.fori_loop(0, TC // UNROLL, spread, 0)
    b_start()
    g_add(1, g_part.at[0])
    g_exchange(2, plane_y, lambda o: g_part.at[1])

    def p_x_landed(j):
        for o in near:
            wire.landed(pxs[j, o], xin.at[o - 1, j], at(dx=-o))
        dsum[j] = total_of([c.at[yy(j), x], xin.at[0, j], xin.at[1, j], xin.at[2, j]])
        if j:
            wire.start(pys[j], dsum.at[j], yin.at[j - 1], at(dyh=j))

    g_add(2, g_part.at[1])
    g_exchange(3, plane_x, lambda o: g_part.at[2])
    p_x_landed(2)
    p_x_landed(1)
    b_middle()
    p_x_landed(3)
    p_x_landed(0)

    for u in (1, 0):
        for d in (1, -1):
            wire.landed(b1s[d, u], b1.at[side[d], u], zdev[-d])
            wire.landed(b2s[d, u], b2.at[side[d], u], at(dz=-2 * d))
        e[u] = total_of([bt_at(0, u), b1.at[0, u], b1.at[1, u], b2.at[0, u], b2.at[1, u]])
        if u == 1:
            wire.start(yls, e.at[1], ylr, ylo)

    for o in near:
        wire.landed(pys[o], yin.at[o - 1], at(dyh=-o))
    agg = total_of([dsum.at[0], yin.at[0], yin.at[1], yin.at[2]])
    layer[...] = lax.dot_general(agg, w[...], TN, preferred_element_type=F32).astype(BF)

    g_landed(3)
    g_in[3, 7] = g_part[2]
    for q in range(N_COL):
        a, h = q // 2, q % 2
        chunk = g_in[3, (m - q // 4 + 7) % 8, q % 4].astype(F32) * scale
        wgrad[a * 16:(a + 1) * 16, h * TILE:(h + 1) * TILE] = chunk

    wire.landed(yls, ylr, ylo)
    mine = total_of([e.at[0], ylr])
    for t in range(TC):
        feat[:, t * TILE:(t + 1) * TILE] = mine[t]

    for stage in range(4):
        sent = g_in.at[stage, pl.ds(0, 7)]
        pltpu.make_async_copy(sent, sent, gsend.at[stage]).wait()
    wire.drain()


def layer_call(xt, w, vals, trow, tcol, live, d_out, scale):
    vmem = pl.BlockSpec(memory_space=pltpu.VMEM)
    here = pl.BlockSpec(memory_space=pltpu.HBM)
    fr = F // N_ROW
    ints = jnp.int32
    return pl.pallas_call(
        functools.partial(layer_kernel, scale),
        out_shape=(
            jax.ShapeDtypeStruct((TILE, F), BF),
            jax.ShapeDtypeStruct((fr, TC * TILE), BF),
            jax.ShapeDtypeStruct((F, F), F32),
        ),
        in_specs=[here] * 7,
        out_specs=(vmem, vmem, vmem),
        scratch_shapes=[
            pltpu.VMEM((N_ROW, F // N_ROW, F), BF),
            pltpu.VMEM((F, F), BF),
            pltpu.VMEM((SLOTS, TILE, TILE), BF),
            pltpu.VMEM((3, 1, SLOTS), ints),
            pltpu.VMEM((8, TILE), ints),
            pltpu.VMEM((8, TILE), ints),
            pltpu.SMEM((8, TILE), ints),
            pltpu.VMEM((fr, TC * TILE), BF),
            pltpu.VMEM((TILE, F), BF),
            pltpu.VMEM((NZ, NYL, TC, fr, TILE), BF),
            pltpu.VMEM((N_COL, F, TILE), BF),
            pltpu.VMEM((SLOTS, F, TILE), BF),
            pltpu.VMEM((NYH, NX, NK, F, TILE), BF),
            pltpu.VMEM((NZ, NYL, TC, fr, TILE), BF),
            pltpu.VMEM((NYH, NX, F, TILE), BF),
            pltpu.VMEM((NYH, NX, F, TILE), BF),
            pltpu.VMEM((NX - 1, NYH, F, TILE), BF),
            pltpu.VMEM((NYH, F, TILE), BF),
            pltpu.VMEM((NYH - 1, F, TILE), BF),
            pltpu.VMEM((2, NYL, TC, fr, TILE), BF),
            pltpu.VMEM((2, NYL, TC, fr, TILE), BF),
            pltpu.VMEM((2, NYL, TC, fr, TILE), BF),
            pltpu.VMEM((2, NYL, TC // 2, fr, TILE), BF),
            pltpu.VMEM((2, NYL, TC, fr, TILE), BF),
            pltpu.VMEM((NYL, TC, fr, TILE), BF),
            pltpu.VMEM((TC, fr, TILE), BF),
            pltpu.VMEM((N_COL, 16, TILE), BF),
            pltpu.VMEM((4, 8, 4, 16, TILE), BF),
            pltpu.VMEM((3, 4, 16, TILE), BF),
            pltpu.SemaphoreType.DMA((7,)),
            pltpu.SemaphoreType.DMA((N_LINK,)),
            pltpu.SemaphoreType.DMA((N_LINK,)),
            pltpu.SemaphoreType.DMA((4,)),
            pltpu.SemaphoreType.DMA((4,)),
        ],
        compiler_params=pltpu.CompilerParams(
            collective_id=0, has_side_effects=True, vmem_limit_bytes=56 << 20),
        name="graph_layer",
    )(xt, w.reshape(N_ROW, fr, F), vals, trow, tcol, live, d_out)


def local(x_feat, weight, tile_vals, tile_row, tile_col, tile_live, d_out):
    nodes = d_out.shape[0] * N_COL * N_ROW
    layer, feat, wgrad = layer_call(
        x_feat.T, weight, tile_vals, tile_row, tile_col, tile_live, d_out, 1.0 / math.sqrt(nodes))
    return layer, wgrad, feat.T


def solution(mesh):
    placed = (
        P("col", "row"),
        P(),
        P("row", "col", None, None, None),
        P("row", "col", None),
        P("row", "col", None),
        P("row", "col", None),
        P(("row", "col"), None),
    )
    return jax.shard_map(
        local,
        mesh=mesh,
        in_specs=placed,
        out_specs=(P(("row", "col"), None), P(), P("col", "row")),
        check_vma=False,
    )
```

```python
import functools
import math

import jax
import jax.numpy as jnp
from jax import lax
from jax.experimental import pallas as pl
from jax.experimental.pallas import tpu as pltpu
from jax.sharding import PartitionSpec as P

TILE = 128
F = 256
NZ, NYL = 8, 2
NYH, NX, NK = 4, 4, 2
N_ROW, N_COL = NZ * NYL, NYH * NX * NK
SLOTS = 96
TR, TC = 32, 16
BF = jnp.bfloat16
F32 = jnp.float32
MESH = pl.DeviceIdType.MESH


def place():
    row, col = lax.axis_index("row"), lax.axis_index("col")
    return row // NYL, row % NYL, col // (NX * NK), (col // NK) % NX, col % NK


class Wire:
    def __init__(self, send, recv):
        self.send, self.recv, self.used, self.started = send, recv, 0, []

    def slot(self):
        self.used += 1
        return self.used - 1

    def start(self, slot, src, dst, device):
        copy = pltpu.make_async_remote_copy(
            src_ref=src, dst_ref=dst, send_sem=self.send.at[slot], recv_sem=self.recv.at[slot],
            device_id=device, device_id_type=MESH)
        copy.start()
        self.started.append(copy)

    def landed(self, slot, dst, device):
        pltpu.make_async_remote_copy(
            src_ref=dst, dst_ref=dst, send_sem=self.send.at[slot], recv_sem=self.recv.at[slot],
            device_id=device, device_id_type=MESH).wait_recv()

    def drain(self):
        for copy in self.started:
            copy.wait_send()


def devices_around():
    z, yl, yh, x, k = place()

    def at(dz=0, dyl=0, dyh=0, dx=0, dk=0):
        row = ((z + dz) % NZ) * NYL + (yl + dyl) % NYL
        col = (((yh + dyh) % NYH) * NX + (x + dx) % NX) * NK + (k + dk) % NK
        return row, col

    return at


N_LINK = 1 + 16 + 3 + 12 + 16 + 4 + 12 + 3 + 16 + 1
UNROLL = 8
RUN = 48
NT = (((1,), (1,)), ((), ()))
TN = (((0,), (0,)), ((), ()))


def total_of(refs):
    out = refs[0][...].astype(F32)
    for ref in refs[1:]:
        out += ref[...].astype(F32)
    return out.astype(BF)


def sorted_rows(key, other, rows):
    shape = (TILE, TILE)
    lane = lax.broadcasted_iota(jnp.int32, shape, 1)
    down = lax.broadcasted_iota(jnp.int32, shape, 0)
    keys = jnp.broadcast_to(key, shape)
    mine = keys * TILE + lane
    theirs = mine.T
    rank = jnp.sum((mine < theirs).astype(jnp.int32), axis=1, keepdims=True)
    hot = rank == lane
    key_down = keys.T
    other_down = jnp.broadcast_to(other, shape).T
    for i, value in enumerate((down, other_down, key_down)):
        rows[i:i + 1, :] = jnp.sum(jnp.where(hot, value, 0), axis=0, keepdims=True)
    rows[3:4, :] = jnp.sum((key_down <= lane).astype(jnp.int32), axis=0, keepdims=True)


def layer_kernel(scale, x_in, w_in, vals_in, idx_in, d_in, layer, feat, wgrad,
                 wl, w, vals, idx, keys, meta_v, meta, xl, dl, xg, dg, runs, pt, bt,
                 core_in, c, xin, dsum, yin, b1, b2, b3, b4, bmid, e, ylr, g, g_in, g_part,
                 loads, send, recv, gsend, grecv):
    z, yl, yh, x, k = place()
    at = devices_around()
    row, col = at()
    wire = Wire(send, recv)
    zdev = {1: at(dz=1), -1: at(dz=-1)}
    sib, ylo = at(dk=1), at(dyl=1)
    barrier = pltpu.get_barrier_semaphore()

    m, n = col % (NX * NK), yh * NYL + yl

    def plane_x(o):
        return row, yh * (NX * NK) + (m + o) % 8

    def plane_y(o):
        there = (n + o) % 8
        return z * NYL + there % NYL, there // NYL * (NX * NK) + m

    def plane_z(o):
        return (z + o) % NZ * NYL + yl, col

    groups = (plane_x, plane_y, plane_z)
    for group in groups:
        for o in range(1, 8):
            pl.semaphore_signal(barrier, inc=1, device_id=group(o), device_id_type=MESH)

    load = [
        pltpu.make_async_copy(src, dst, loads.at[i])
        for i, (src, dst) in enumerate((
            (x_in, xl), (d_in, dl),
            (idx_in, idx),
            (w_in, wl), (vals_in.at[0, 0], vals)))
    ]
    for copy in load:
        copy.start()
    load[0].wait()
    for t in range(TC):
        xg[1, 0, t] = xl[:, t * TILE:(t + 1) * TILE]
    load[1].wait()
    dg[col] = dl[...].astype(F32).T.astype(BF)
    pl.semaphore_wait(barrier, 7 * len(groups))

    ys = wire.slot()
    zs = {(d, s, u): wire.slot() for d in (1, -1) for s in (1, 2, 3, 4) for u in (0, 1)}
    half = {1: pl.ds(0, TC // 2), -1: pl.ds(TC // 2, TC // 2)}

    def xpart(dz, u, d, s):
        ref = xg.at[(dz + 1) % NZ, u]
        return ref.at[half[d]] if s == 4 else ref

    def z_send(d, s, u):
        hop = s if s < 3 else s - 2
        back = 0 if s < 3 else -2 * d
        wire.start(zs[d, s, u], xpart(back, u, d, s), xpart(-d * s, u, d, s), at(dz=hop * d))

    def z_landed(d, s, u):
        hop = s if s < 3 else s - 2
        wire.landed(zs[d, s, u], xpart(-d * s, u, d, s), at(dz=-hop * d))

    def z_first(u):
        for s in (2, 1):
            for d in (1, -1):
                z_send(d, s, u)

    def z_second(u):
        for d in (1, -1):
            z_landed(d, 2, u)
            for s in (3, 4):
                z_send(d, s, u)

    def z_third():
        for s in (1, 3, 4):
            for u in (0, 1):
                for d in (1, -1):
                    z_landed(d, s, u)

    def piece(j, dx=0, dk=0):
        return dg.at[at(dyh=j, dx=dx, dk=dk)[1]]

    dys = {o: wire.slot() for o in (1, 3, 2)}
    dxs = {(j, o): wire.slot() for j in range(4) for o in (1, 3, 2)}
    dks = {(j, dx): wire.slot() for j in range(4) for dx in range(4)}

    def d_to_x(j):
        for o in (1, 3, 2):
            wire.start(dxs[j, o], piece(j), piece(j), at(dx=o))
        wire.start(dks[j, 0], piece(j), piece(j), sib)

    def d_x_landed(j):
        for o in (1, 3, 2):
            part = piece(j, -o)
            wire.landed(dxs[j, o], part, at(dx=-o))
            wire.start(dks[j, -o % 4], part, part, sib)

    mine = xg.at[1, 0]
    z_first(0)
    wire.start(ys, mine, xg.at[1, 1], ylo)
    for o in (1, 3, 2):
        wire.start(dys[o], piece(0), piece(0), at(dyh=o))
    d_to_x(0)

    load[2].wait()
    keys[...] = jnp.full(keys.shape, TILE - 1, jnp.int32)
    keys[0:3, 0:SLOTS] = idx[...]
    alive = keys[2:3, :] > 0
    sorted_rows(jnp.where(alive, keys[0:1, :], TR), keys[1:2, :], meta_v.at[0:4])
    wire.landed(ys, xg.at[1, 1], ylo)
    z_first(1)
    sorted_rows(jnp.where(alive, keys[1:2, :], TC), keys[0:1, :], meta_v.at[4:8])
    to_scalars = pltpu.make_async_copy(meta_v, meta, loads.at[0])
    to_scalars.start()

    z_second(0)
    for o in (1, 3):
        wire.landed(dys[o], piece(-o), at(dyh=-o))
        d_to_x(-o % 4)
    z_second(1)
    wire.landed(dys[2], piece(2), at(dyh=2))
    d_to_x(2)
    d_x_landed(0)
    load[3].wait()
    for i in range(NZ):
        for u in (0, 1):
            b = (i * NYL + u) * (F // N_ROW)
            w[b:b + F // N_ROW, :] = wl[at(dz=i - 1, dyl=u)[0]]
    to_scalars.wait()
    load[4].wait()

    def run(base, source, contract, begin=0, end=SLOTS // RUN, acc=None):
        def step(i, acc):
            for v in range(RUN):
                s = i * RUN + v
                slot, other = meta[base, s], meta[base + 1, s]
                same = jnp.logical_and(s > 0, meta[base + 2, s] == meta[base + 2, jnp.maximum(s - 1, 0)])
                prod = lax.dot_general(source(other), vals[slot], contract, preferred_element_type=F32)
                acc = jnp.where(same, acc + prod, prod)
                runs[s] = acc.astype(BF)
            return acc
        acc = jnp.zeros((F, TILE), F32) if acc is None else acc
        return lax.fori_loop(begin, end, step, acc)

    def last_of(base, t):
        count = meta[base + 3, t]
        before = jnp.where(t > 0, meta[base + 3, jnp.maximum(t - 1, 0)], 0)
        value = runs[jnp.maximum(count - 1, 0)]
        return jnp.where(count > before, value, jnp.zeros_like(value))

    z_third()
    run(0, lambda i: xg[:, :, i].reshape(F, TILE), NT)

    order = (2, 1, 3, 0)
    near = (1, 3, 2)

    def yy(j):
        return (yh + j) % NYH

    cs = {j: wire.slot() for j in order}
    pxs = {(j, o): wire.slot() for j in order for o in near}
    pys = {o: wire.slot() for o in near}

    def fill(core):
        def one(i, carry):
            for v in range(NX):
                pt[i, v, core] = last_of(0, (i * NX + v) * NK + core)
            return carry
        return one

    lax.fori_loop(0, NYH, fill(1 - k), 0)
    for j in order:
        wire.start(cs[j], pt.at[yy(j), :, 1 - k], core_in.at[yy(j)], sib)

    for j in (3, 1, 2):
        d_x_landed(j)
    lax.fori_loop(0, NYH, fill(k), 0)

    b1s, b2s, b3s, b4s = ({(d, u): wire.slot() for d in (1, -1) for u in (0, 1)} for _ in range(4))
    side = {1: 0, -1: 1}
    yls = wire.slot()

    def bt_at(dz, u):
        return bt.at[(dz + 1) % NZ, u]

    def b_start():
        for u in (1, 0):
            for d in (1, -1):
                wire.start(b3s[d, u], bt_at(3 * d, u), b3.at[side[d], u], zdev[d])
                wire.start(b4s[d, u], bt_at(4, u).at[half[d]], b4.at[side[d], u], at(dz=2 * d))
        for u in (1, 0):
            for d in (1, -1):
                wire.start(b1s[d, u], bt_at(d, u), b1.at[side[d], u], zdev[d])

    def b_middle():
        for u in (1, 0):
            for d in (1, -1):
                wire.landed(b3s[d, u], b3.at[side[d], u], zdev[-d])
                wire.landed(b4s[d, u], b4.at[side[d], u], at(dz=-2 * d))
                mid, own = bmid.at[side[d], u], bt_at(2 * d, u)
                mid[half[-d]] = total_of([own.at[half[-d]], b3.at[side[d], u, half[-d]]])
                mid[half[d]] = total_of([own.at[half[d]], b3.at[side[d], u, half[d]], b4.at[side[d], u]])
                wire.start(b2s[d, u], mid, b2.at[side[d], u], at(dz=2 * d))

    def spread(i, carry):
        for v in range(UNROLL):
            t = i * UNROLL + v
            term = jnp.dot(w[...], last_of(4, t), preferred_element_type=F32)
            bt[:, :, t] = term.astype(BF).reshape(NZ, NYL, F // N_ROW, TILE)
        return carry

    for j in order:
        wire.landed(cs[j], core_in.at[yy(j)], sib)

        def add(i, carry):
            c[yy(j), i] = total_of([pt.at[yy(j), i, k], core_in.at[yy(j), i]])
            return carry

        lax.fori_loop(0, NX, add, 0)

    def grad_term(i, total):
        for v in range(NX):
            total += lax.dot_general(
                c[i, v], dg[(i * NX + v) * NK + k], NT, preferred_element_type=F32)
        return total

    total = lax.fori_loop(0, NYH, grad_term, jnp.zeros((F, F), F32)).astype(BF)
    for i in range(NZ):
        for u in (0, 1):
            b, a = (i * NYL + u) * 16, at(dz=i - 1, dyl=u)[0]
            for h in (0, 1):
                g[2 * a + h] = total[b:b + 16, h * TILE:(h + 1) * TILE]

    def g_exchange(stage, group, source):
        for o in range(1, 8):
            pltpu.make_async_remote_copy(
                src_ref=source(o), dst_ref=g_in.at[stage, o - 1],
                send_sem=gsend.at[stage], recv_sem=grecv.at[stage],
                device_id=group(o), device_id_type=MESH).start()

    def g_landed(stage):
        landing = g_in.at[stage, pl.ds(0, 7)]
        pltpu.make_async_copy(landing, landing, grecv.at[stage]).wait()

    def g_add(stage, own):
        g_landed(stage)
        g_part[stage] = (jnp.sum(g_in[stage, 0:7].astype(F32), axis=0) + own[...].astype(F32)).astype(BF)

    g_exchange(0, plane_x, lambda o: g.at[pl.ds((m + o) % 8 * 4, 4)])

    for j in order:
        for o in near:
            wire.start(pxs[j, o], c.at[yy(j), (x + o) % NX], xin.at[o - 1, j], at(dx=o))

    for j in (0, 3, 1, 2):
        for dx in range(4):
            wire.landed(dks[j, dx], piece(j, dx, 1), sib)

    part = run(4, lambda i: dg[i], (((1,), (0,)), ((), ())), 0, 1)
    g_add(0, g.at[pl.ds(m * 4, 4)])
    g_exchange(1, plane_z, lambda o: g_part.at[0])
    run(4, lambda i: dg[i], (((1,), (0,)), ((), ())), 1, SLOTS // RUN, part)
    lax.fori_loop(0, TC // UNROLL, spread, 0)
    b_start()
    g_add(1, g_part.at[0])
    g_exchange(2, plane_y, lambda o: g_part.at[1])

    def p_x_landed(j):
        for o in near:
            wire.landed(pxs[j, o], xin.at[o - 1, j], at(dx=-o))
        dsum[j] = total_of([c.at[yy(j), x], xin.at[0, j], xin.at[1, j], xin.at[2, j]])
        if j:
            wire.start(pys[j], dsum.at[j], yin.at[j - 1], at(dyh=j))

    g_add(2, g_part.at[1])
    g_exchange(3, plane_x, lambda o: g_part.at[2])
    p_x_landed(2)
    p_x_landed(1)
    b_middle()
    p_x_landed(3)
    p_x_landed(0)

    for u in (1, 0):
        for d in (1, -1):
            wire.landed(b1s[d, u], b1.at[side[d], u], zdev[-d])
            wire.landed(b2s[d, u], b2.at[side[d], u], at(dz=-2 * d))
        e[u] = total_of([bt_at(0, u), b1.at[0, u], b1.at[1, u], b2.at[0, u], b2.at[1, u]])
        if u == 1:
            wire.start(yls, e.at[1], ylr, ylo)

    for o in near:
        wire.landed(pys[o], yin.at[o - 1], at(dyh=-o))
    agg = total_of([dsum.at[0], yin.at[0], yin.at[1], yin.at[2]])
    layer[...] = lax.dot_general(agg, w[...], TN, preferred_element_type=F32).astype(BF)

    g_landed(3)
    g_in[3, 7] = g_part[2]
    for q in range(N_COL):
        a, h = q // 2, q % 2
        chunk = g_in[3, (m - q // 4 + 7) % 8, q % 4].astype(F32) * scale
        wgrad[a * 16:(a + 1) * 16, h * TILE:(h + 1) * TILE] = chunk

    wire.landed(yls, ylr, ylo)
    mine = total_of([e.at[0], ylr])
    for t in range(TC):
        feat[:, t * TILE:(t + 1) * TILE] = mine[t]

    for stage in range(4):
        sent = g_in.at[stage, pl.ds(0, 7)]
        pltpu.make_async_copy(sent, sent, gsend.at[stage]).wait()
    wire.drain()


def layer_call(xt, w, vals, idx, d_out, scale):
    vmem = pl.BlockSpec(memory_space=pltpu.VMEM)
    here = pl.BlockSpec(memory_space=pltpu.HBM)
    fr = F // N_ROW
    ints = jnp.int32
    return pl.pallas_call(
        functools.partial(layer_kernel, scale),
        out_shape=(
            jax.ShapeDtypeStruct((TILE, F), BF),
            jax.ShapeDtypeStruct((fr, TC * TILE), BF),
            jax.ShapeDtypeStruct((F, F), F32),
        ),
        in_specs=[here] * 5,
        out_specs=(vmem, vmem, vmem),
        scratch_shapes=[
            pltpu.VMEM((N_ROW, F // N_ROW, F), BF),
            pltpu.VMEM((F, F), BF),
            pltpu.VMEM((SLOTS, TILE, TILE), BF),
            pltpu.VMEM((3, SLOTS), ints),
            pltpu.VMEM((8, TILE), ints),
            pltpu.VMEM((8, TILE), ints),
            pltpu.SMEM((8, TILE), ints),
            pltpu.VMEM((fr, TC * TILE), BF),
            pltpu.VMEM((TILE, F), BF),
            pltpu.VMEM((NZ, NYL, TC, fr, TILE), BF),
            pltpu.VMEM((N_COL, F, TILE), BF),
            pltpu.VMEM((SLOTS, F, TILE), BF),
            pltpu.VMEM((NYH, NX, NK, F, TILE), BF),
            pltpu.VMEM((NZ, NYL, TC, fr, TILE), BF),
            pltpu.VMEM((NYH, NX, F, TILE), BF),
            pltpu.VMEM((NYH, NX, F, TILE), BF),
            pltpu.VMEM((NX - 1, NYH, F, TILE), BF),
            pltpu.VMEM((NYH, F, TILE), BF),
            pltpu.VMEM((NYH - 1, F, TILE), BF),
            pltpu.VMEM((2, NYL, TC, fr, TILE), BF),
            pltpu.VMEM((2, NYL, TC, fr, TILE), BF),
            pltpu.VMEM((2, NYL, TC, fr, TILE), BF),
            pltpu.VMEM((2, NYL, TC // 2, fr, TILE), BF),
            pltpu.VMEM((2, NYL, TC, fr, TILE), BF),
            pltpu.VMEM((NYL, TC, fr, TILE), BF),
            pltpu.VMEM((TC, fr, TILE), BF),
            pltpu.VMEM((N_COL, 16, TILE), BF),
            pltpu.VMEM((4, 8, 4, 16, TILE), BF),
            pltpu.VMEM((3, 4, 16, TILE), BF),
            pltpu.SemaphoreType.DMA((5,)),
            pltpu.SemaphoreType.DMA((N_LINK,)),
            pltpu.SemaphoreType.DMA((N_LINK,)),
            pltpu.SemaphoreType.DMA((4,)),
            pltpu.SemaphoreType.DMA((4,)),
        ],
        compiler_params=pltpu.CompilerParams(
            collective_id=0, has_side_effects=True, vmem_limit_bytes=55040 << 10),
        name="graph_layer",
    )(xt, w.reshape(N_ROW, fr, F), vals, idx, d_out)


def local(x_feat, weight, tile_vals, tile_row, tile_col, tile_live, d_out):
    nodes = d_out.shape[0] * N_COL * N_ROW
    idx = jnp.concatenate([tile_row[0], tile_col[0], tile_live[0]], axis=0)
    layer, feat, wgrad = layer_call(
        x_feat.T, weight, tile_vals, idx, d_out, 1.0 / math.sqrt(nodes))
    return layer, wgrad, feat.T


def solution(mesh):
    placed = (
        P("col", "row"),
        P(),
        P("row", "col", None, None, None),
        P("row", "col", None),
        P("row", "col", None),
        P("row", "col", None),
        P(("row", "col"), None),
    )
    return jax.shard_map(
        local,
        mesh=mesh,
        in_specs=placed,
        out_specs=(P(("row", "col"), None), P(), P("col", "row")),
        check_vma=False,
    )
```
